32 devices in a mesh: tp: 8 (over y, x, core), sp: 4 (over z).
Axes of the slice: x: 2, y: 2, z: 4, core: 2. Of those that a mesh axis runs over, the one named last changes fastest.
Arguments:
- inputs: bfloat16 [256, 8192], P('tp', 'sp'), may hold values from -6 to 6
- out_grad: bfloat16 [256, 8192], P('sp', 'tp'), may hold values from -6 to 6
- gate_pre: bfloat16 [256, 28672], P(None, 'tp'), may hold values from -6 to 6
- up_pre: bfloat16 [256, 28672], P(None, 'tp'), may hold values from -6 to 6
- w_gate: bfloat16 [8192, 28672], P('sp', 'tp'), may hold values from -0.0625 to 0.0625
- w_up: bfloat16 [8192, 28672], P('sp', 'tp'), may hold values from -0.0625 to 0.0625
- w_down: bfloat16 [28672, 8192], P('tp', 'sp'), may hold values from -0.03125 to 0.03125
Outputs:
- grad_input: bfloat16 [256, 8192], P('tp', 'sp')
- grad_gate: bfloat16 [8192, 28672], P('sp', 'tp')
- grad_up: bfloat16 [8192, 28672], P('sp', 'tp')
- grad_down: bfloat16 [28672, 8192], P('tp', 'sp')
The draws below stay inside these ranges and needn't reach their ends.
All inputs are finite; a program needn't handle non-finite values.
Results may differ from the reference program's by a relative error of at most 0.0049.
Values may be sent and summed in bfloat16 or wider, within the bound.
A program may use at most 192 MiB of HBM per device.

```python
import jax
import jax.numpy as jnp

D = 8192
FF = 28672
TOKENS = 256


def block_levels(stream_key, dims, split, least, high):
    factor_of = 1.0
    for dim, blocks in split:
        heights = jax.random.uniform(jax.random.fold_in(jax.random.fold_in(stream_key, 6), dim), (blocks,), jnp.float32, least / len(split), high / len(split))
        factor_of = factor_of * jnp.repeat(jnp.exp(heights), dims[dim] // blocks).reshape((-1,) + (1,) * (len(dims) - 1 - dim))
    return factor_of


def centred(key, shape, width, most, split=(), held_as=jnp.bfloat16):
    result = width * jax.random.normal(key, shape, jnp.float32)
    if split:
        result = result * block_levels(key, shape, split, -0.22, 0.18)
    return jnp.clip(result, -most, most).astype(held_as)


def setup_inputs(seed: int = 0) -> dict:
    streams_of = jax.random.split(jax.random.key(seed), 8)
    return {
        "inputs": centred(streams_of[0], (TOKENS, D), 1.0, 6.0, ((0, 8), (1, 4))),
        "out_grad": centred(streams_of[1], (TOKENS, D), 1.0, 6.0, ((0, 4), (1, 8))),
        "gate_pre": centred(streams_of[2], (TOKENS, FF), 1.5, 6.0, ((1, 8),)),
        "up_pre": centred(streams_of[3], (TOKENS, FF), 1.0, 6.0, ((1, 8),)),
        "w_gate": centred(streams_of[4], (D, FF), D ** -0.5, 0.0625, ((0, 4), (1, 8))),
        "w_up": centred(streams_of[5], (D, FF), D ** -0.5, 0.0625, ((0, 4), (1, 8))),
        "w_down": centred(streams_of[6], (FF, D), FF ** -0.5, 0.03125, ((0, 8), (1, 4))),
    }


def reference(inputs, out_grad, gate_pre, up_pre, w_gate, w_up, w_down):
    gate = gate_pre.astype(jnp.float32)
    upward = up_pre.astype(jnp.float32)
    sigmoid = jax.nn.sigmoid(gate)
    swish = gate * sigmoid
    hidden = (swish * upward).astype(jnp.bfloat16)
    hidden_grad = jnp.dot(out_grad, w_down.T, preferred_element_type=jnp.float32)
    up_grad = (hidden_grad * swish).astype(jnp.bfloat16)
    gate_grad = (hidden_grad * upward * sigmoid * (1.0 + gate * (1.0 - sigmoid))).astype(jnp.bfloat16)
    grad_down = jnp.dot(hidden.T, out_grad, preferred_element_type=jnp.float32).astype(jnp.bfloat16)
    grad_gate = jnp.dot(inputs.T, gate_grad, preferred_element_type=jnp.float32).astype(jnp.bfloat16)
    grad_up = jnp.dot(inputs.T, up_grad, preferred_element_type=jnp.float32).astype(jnp.bfloat16)
    total = jnp.dot(gate_grad, w_gate.T, preferred_element_type=jnp.float32)
    total = total + jnp.dot(up_grad, w_up.T, preferred_element_type=jnp.float32)
    return total.astype(jnp.bfloat16), grad_gate, grad_up, grad_down
```

```python
import functools

import jax
import jax.numpy as jnp
from jax import lax
from jax.experimental import pallas as pl
from jax.experimental.pallas import tpu as pltpu
from jax.sharding import PartitionSpec as P

BF = jnp.bfloat16
F32 = jnp.float32
MESH = pl.DeviceIdType.MESH
ANY = pl.BlockSpec(memory_space=pl.ANY)
VM = pl.BlockSpec(memory_space=pltpu.VMEM)
SLOTS = 4


def swiglu_back(hidden_grad, gate_pre, up_pre):
    gate = gate_pre.astype(F32)
    upward = up_pre.astype(F32)
    sigmoid = jax.nn.sigmoid(gate)
    up_grad = (hidden_grad * gate * sigmoid).astype(BF)
    gate_grad = (hidden_grad * upward * sigmoid * (1.0 + gate * (1.0 - sigmoid))).astype(BF)
    return (gate_grad, up_grad)


def rows_times(grads, weight):
    return lax.dot_general(grads, weight, (((1,), (1,)), ((), ())), preferred_element_type=F32)


def plain(inputs, out_grad, gate_pre, up_pre, w_gate, w_up, w_down):
    wide_rows = lax.all_gather(out_grad, "tp", axis=1, tiled=True)
    regrouped = lax.all_to_all(wide_rows, "sp", split_axis=1, concat_axis=0, tiled=True)
    gate = gate_pre.astype(F32)
    hidden = (gate * jax.nn.sigmoid(gate) * up_pre.astype(F32)).astype(BF)
    grad_down = lax.dot_general(
        hidden, regrouped, (((0,), (0,)), ((), ())), preferred_element_type=F32
    ).astype(BF)
    partial_grad = rows_times(regrouped, w_down)
    hidden_grad = lax.psum(partial_grad, "sp")
    gate_grad, up_grad = swiglu_back(hidden_grad, gate_pre, up_pre)
    dims = (((0,), (0,)), ((), ()))
    piece = lax.all_gather(inputs, "tp", axis=0, tiled=True)
    new_gate = lax.dot_general(piece, gate_grad, dims, preferred_element_type=F32)
    new_up = lax.dot_general(piece, up_grad, dims, preferred_element_type=F32)
    via_gate = lax.psum_scatter(
        rows_times(gate_grad, w_gate), "tp", scatter_dimension=0, tiled=True
    )
    via_up = lax.psum_scatter(rows_times(up_grad, w_up), "tp", scatter_dimension=0, tiled=True)
    total = via_gate + via_up
    return (total.astype(BF), new_gate.astype(BF), new_up.astype(BF), grad_down)


def first_kernel(
    n_q, n_s, chunk, n_c, tile,
    inputs, out_grad, gate_pre, up_pre, w_gate, w_up, w_down,
    grad_in, x_out, in_t_out, gg_out, ug_out, hid_out,
    quarter, x_all, x_flat, in_all, in_t, w_d, w_gu, part,
    from_l, from_r, to_r, to_l, gates, ups, gg, ug, hid, g_in, half_in, block_out, block_in,
    sem_a, sem_b, sem_c, sem_d, sem_i, sem_j, sem_h, sem_e,
    sem_wd, sem_w, sem_gu, sem_r, sem_l, sem_out, sem_x,
):
    t = lax.axis_index("tp")
    s = lax.axis_index("sp")
    q = t // 2
    k = lax.rem(t, 2)
    mate = t + 1 - 2 * k
    rows16 = quarter.shape[1]
    half = quarter.shape[2]
    depth = x_flat.shape[1]
    tokens = x_flat.shape[0]
    cols = pl.ds(pl.multiple_of(k * half, half), half)

    def wd_copy(j):
        return pltpu.make_async_copy(
            w_down.at[pl.ds(pl.multiple_of(j * chunk, chunk), chunk)], w_d.at[j], sem_wd.at[j]
        )

    def col(j):
        return pl.ds(pl.multiple_of(j * chunk, chunk), chunk)

    def w_copies(j):
        slot = lax.rem(j, SLOTS)
        return (
            pltpu.make_async_copy(
                w_gate.at[:, col(j)], w_gu.at[slot, :, pl.ds(0, chunk)], sem_w.at[0, slot]
            ),
            pltpu.make_async_copy(
                w_up.at[:, col(j)], w_gu.at[slot, :, pl.ds(chunk, chunk)], sem_w.at[1, slot]
            ),
        )

    def pre_copies(j):
        return (
            pltpu.make_async_copy(gate_pre.at[:, col(j)], gates.at[j], sem_gu.at[0, j]),
            pltpu.make_async_copy(up_pre.at[:, col(j)], ups.at[j], sem_gu.at[1, j]),
        )

    def out_copies(j):
        return (
            pltpu.make_async_copy(gg.at[j], gg_out.at[j], sem_out.at[0, j]),
            pltpu.make_async_copy(ug.at[j], ug_out.at[j], sem_out.at[1, j]),
            pltpu.make_async_copy(hid.at[j], hid_out.at[j], sem_out.at[2, j]),
        )

    def remote(src, dst, sems, at, where):
        return pltpu.make_async_remote_copy(
            src_ref=src, dst_ref=dst, send_sem=sems.at[(0, *at)], recv_sem=sems.at[(1, *at)],
            device_id=where, device_id_type=MESH,
        )

    barrier = pltpu.get_barrier_semaphore()
    for o in range(1, n_q):
        pl.semaphore_signal(
            barrier, inc=1, device_id={"tp": lax.rem(q + o, n_q) * 2 + k}, device_id_type=MESH
        )
    for o in range(1, n_s):
        pl.semaphore_signal(
            barrier, inc=1, device_id={"sp": lax.rem(s + o, n_s)}, device_id_type=MESH
        )
    pl.semaphore_signal(barrier, inc=1, device_id={"tp": mate}, device_id_type=MESH)

    @pl.loop(0, n_c)
    def _(j):
        wd_copy(j).start()

    pl.semaphore_wait(barrier, n_q + n_s - 1)

    stage = []
    for o in range(1, n_q):
        peer = lax.rem(q + o, n_q)
        stage.append(
            remote(
                out_grad.at[pl.ds(pl.multiple_of(peer * rows16, rows16), rows16)],
                quarter.at[q], sem_a, (o,), {"tp": peer * 2 + k},
            )
        )
        stage[-1].start()
    quarter[q] = out_grad[pl.ds(pl.multiple_of(q * rows16, rows16), rows16), :]
    for c in stage:
        c.wait()
    stage = []
    for o in range(1, n_s):
        peer = lax.rem(s + o, n_s)
        stage.append(
            remote(quarter.at[peer], x_all.at[s, q, :, cols], sem_b, (o,), {"sp": peer})
        )
        stage[-1].start()
    x_all[s, q, :, cols] = quarter[s]
    for c in stage:
        c.wait()
    stage = []
    for o in range(1, n_q):
        peer = lax.rem(q + o, n_q)
        stage.append(
            remote(
                x_all.at[:, q, :, cols], x_all.at[:, q, :, cols], sem_c, (o,),
                {"tp": peer * 2 + k},
            )
        )
        stage[-1].start()

    @pl.loop(0, n_c)
    def _(j):
        for c in pre_copies(j):
            c.start()

    for j in range(min(SLOTS, n_c)):
        for c in w_copies(j):
            c.start()
    for c in stage:
        c.wait()
    swap = remote(x_all.at[:, :, :, cols], x_all.at[:, :, :, cols], sem_d, (0,), {"tp": mate})
    swap.start()
    in_stage = []
    for o in range(1, n_q):
        peer = lax.rem(q + o, n_q)
        in_stage.append(
            remote(inputs, in_all.at[q, k], sem_i, (o,), {"tp": peer * 2 + k})
        )
        in_stage[-1].start()
    in_all[q, k] = inputs[...]
    g_in[...] = jnp.zeros_like(g_in)
    swap.wait()
    x_flat[...] = x_all[...].reshape(tokens, depth)
    x_copy = pltpu.make_async_copy(x_flat, x_out, sem_x.at[0])
    x_copy.start()

    def send_r(j):
        return remote(
            to_r.at[j], from_l.at[j], sem_r, (j,), {"sp": jnp.minimum(s + 1, n_s - 1)}
        )

    def send_l(j):
        return remote(to_l.at[j], from_r.at[j], sem_l, (j,), {"sp": jnp.maximum(s - 1, 0)})

    @pl.loop(0, n_c)
    def _(j):
        wd_copy(j).wait()
        p = lax.dot_general(
            x_flat[...], w_d[j], (((1,), (1,)), ((), ())), preferred_element_type=F32
        )
        part[j] = p

        @pl.when(s == 0)
        def _():
            to_r[j] = p.astype(BF)
            send_r(j).start()
            from_l[j] = jnp.zeros((tokens, chunk), BF)

        @pl.when(s == n_s - 1)
        def _():
            to_l[j] = p.astype(BF)
            send_l(j).start()
            from_r[j] = jnp.zeros((tokens, chunk), BF)

    for c in in_stage:
        c.wait()
    in_swap = remote(in_all.at[:, k], in_all.at[:, k], sem_j, (0,), {"tp": mate})
    in_swap.start()

    lag = jnp.maximum(s - 1, n_s - 2 - s)

    def finish(f):
        for c in pre_copies(f):
            c.wait()
        h = part[f] + from_l[f].astype(F32) + from_r[f].astype(F32)
        gate = gates[f].astype(F32)
        upward = ups[f].astype(F32)
        sigmoid = 1.0 / (1.0 + jnp.exp(-gate))
        swish = gate * sigmoid
        gg[f] = (h * upward * sigmoid * (1.0 + gate * (1.0 - sigmoid))).astype(BF)
        ug[f] = (h * swish).astype(BF)
        hid[f] = (swish * upward).astype(BF).T
        for c in out_copies(f):
            c.start()
        for c in w_copies(f):
            c.wait()
        slot = lax.rem(f, SLOTS)

        @pl.loop(0, depth // tile)
        def _(i):
            at = pl.ds(pl.multiple_of(i * tile, tile), tile)
            w = w_gu[slot, at, :]
            d = lax.dot_general(
                gg[f], w[:, :chunk], (((1,), (1,)), ((), ())), preferred_element_type=F32
            ) + lax.dot_general(
                ug[f], w[:, chunk:], (((1,), (1,)), ((), ())), preferred_element_type=F32
            )
            g_in[:, :, :, at] += d.reshape(n_q, 2, tokens // (2 * n_q), tile)

        @pl.when(f + SLOTS < n_c)
        def _():
            for c in w_copies(f + SLOTS):
                c.start()

    @pl.loop(0, n_c + n_s - 2)
    def _(step):
        cr = step - (s - 1)
        cl = step - (n_s - 2 - s)
        f = step - lag

        @pl.when((s > 0) & (cr >= 0) & (cr < n_c))
        def _():
            send_r(cr).wait_recv()

            @pl.when(s < n_s - 1)
            def _():
                to_r[cr] = (part[cr] + from_l[cr].astype(F32)).astype(BF)
                send_r(cr).start()

        @pl.when((s < n_s - 1) & (cl >= 0) & (cl < n_c))
        def _():
            send_l(cl).wait_recv()

            @pl.when(s > 0)
            def _():
                to_l[cl] = (part[cl] + from_r[cl].astype(F32)).astype(BF)
                send_l(cl).start()

        @pl.when((f >= 0) & (f < n_c))
        def _():
            finish(f)

        @pl.when(step == n_c // 2)
        def _():
            in_swap.wait()
            in_t[...] = in_all[...].reshape(tokens, depth).T
            pltpu.make_async_copy(in_t, in_t_out, sem_x.at[1]).start()

    pair = remote(g_in.at[:, 1 - k], half_in, sem_h, (0,), {"tp": mate})
    pair.start()
    pair.wait()
    stage = []
    for o in range(1, n_q):
        peer = lax.rem(q + o, n_q)
        block_out[o] = (g_in[peer, k] + half_in[peer]).astype(BF)
        stage.append(
            remote(block_out.at[o], block_in.at[o], sem_e, (o,), {"tp": peer * 2 + k})
        )
        stage[-1].start()
    total = g_in[q, k] + half_in[q]

    @pl.loop(0, n_c)
    def _(j):
        for c in out_copies(j):
            c.wait()

        @pl.when(s < n_s - 1)
        def _():
            send_r(j).wait_send()

        @pl.when(s > 0)
        def _():
            send_l(j).wait_send()

    x_copy.wait()
    pltpu.make_async_copy(in_t, in_t_out, sem_x.at[1]).wait()
    for c in stage:
        c.wait()
    for o in range(1, n_q):
        total = total + block_in[o].astype(F32)
    grad_in[...] = total.astype(BF)


def second_kernel(n_sub, chunk, x, in_t, gg, ug, hid, d_gate, d_up, d_down):
    for c in range(n_sub):
        at = slice(c * chunk, (c + 1) * chunk)
        d_gate[:, at] = jnp.dot(in_t[...], gg[c], preferred_element_type=F32).astype(BF)
        d_up[:, at] = jnp.dot(in_t[...], ug[c], preferred_element_type=F32).astype(BF)
        d_down[at, :] = jnp.dot(hid[c], x[...], preferred_element_type=F32).astype(BF)


def fused(n_q, n_s, chunk, inputs, out_grad, gate_pre, up_pre, w_gate, w_up, w_down):
    rows, depth = inputs.shape
    tokens, units = gate_pre.shape
    n_c = units // chunk
    half = depth // 2
    rows16 = out_grad.shape[0] // n_q
    tile = min(512, depth)
    sds = jax.ShapeDtypeStruct
    dma = pltpu.SemaphoreType.DMA
    vm = pltpu.VMEM
    scratch = [
        vm((n_q, rows16, half), BF),
        vm((n_s, n_q, rows16, depth), BF),
        vm((tokens, depth), BF),
        vm((n_q, 2, rows, depth), BF),
        vm((depth, tokens), BF),
        vm((n_c, chunk, depth), BF),
        vm((SLOTS, depth, 2 * chunk), BF),
        vm((n_c, tokens, chunk), F32),
        vm((n_c, tokens, chunk), BF),
        vm((n_c, tokens, chunk), BF),
        vm((n_c, tokens, chunk), BF),
        vm((n_c, tokens, chunk), BF),
        vm((n_c, tokens, chunk), BF),
        vm((n_c, tokens, chunk), BF),
        vm((n_c, tokens, chunk), BF),
        vm((n_c, tokens, chunk), BF),
        vm((n_c, chunk, tokens), BF),
        vm((n_q, 2, rows, depth), F32),
        vm((n_q, rows, depth), F32),
        vm((n_q, rows, depth), BF),
        vm((n_q, rows, depth), BF),
        dma((2, n_q)),
        dma((2, n_s)),
        dma((2, n_q)),
        dma((2, 1)),
        dma((2, n_q)),
        dma((2, 1)),
        dma((2, 1)),
        dma((2, n_q)),
        dma((n_c,)),
        dma((2, SLOTS)),
        dma((2, n_c)),
        dma((2, n_c)),
        dma((2, n_c)),
        dma((3, n_c)),
        dma((2,)),
    ]
    grad_in, x, in_t, gg, ug, hid = pl.pallas_call(
        functools.partial(first_kernel, n_q, n_s, chunk, n_c, tile),
        out_shape=(
            sds((rows, depth), BF),
            sds((tokens, depth), BF),
            sds((depth, tokens), BF),
            sds((n_c, tokens, chunk), BF),
            sds((n_c, tokens, chunk), BF),
            sds((n_c, chunk, tokens), BF),
        ),
        in_specs=[VM, VM, ANY, ANY, ANY, ANY, ANY],
        out_specs=(VM, ANY, ANY, ANY, ANY, ANY),
        scratch_shapes=scratch,
        compiler_params=pltpu.CompilerParams(
            collective_id=0, has_side_effects=True, vmem_limit_bytes=60 * 1024 * 1024
        ),
        cost_estimate=pl.CostEstimate(
            flops=6 * tokens * depth * units,
            bytes_accessed=6 * depth * units + 14 * tokens * units,
            transcendentals=tokens * units,
        ),
    )(inputs, out_grad, gate_pre, up_pre, w_gate, w_up, w_down)

    n_sub = 2 if n_c % 2 == 0 else 1
    wide = n_sub * chunk
    whole = lambda i: (0, 0)
    d_gate, d_up, d_down = pl.pallas_call(
        functools.partial(second_kernel, n_sub, chunk),
        grid=(n_c // n_sub,),
        out_shape=(
            sds((depth, units), BF),
            sds((depth, units), BF),
            sds((units, depth), BF),
        ),
        in_specs=[
            pl.BlockSpec((tokens, depth), whole),
            pl.BlockSpec((depth, tokens), whole),
            pl.BlockSpec((n_sub, tokens, chunk), lambda i: (i, 0, 0)),
            pl.BlockSpec((n_sub, tokens, chunk), lambda i: (i, 0, 0)),
            pl.BlockSpec((n_sub, chunk, tokens), lambda i: (i, 0, 0)),
        ],
        out_specs=(
            pl.BlockSpec((depth, wide), lambda i: (0, i)),
            pl.BlockSpec((depth, wide), lambda i: (0, i)),
            pl.BlockSpec((wide, depth), lambda i: (i, 0)),
        ),
        compiler_params=pltpu.CompilerParams(vmem_limit_bytes=60 * 1024 * 1024),
        cost_estimate=pl.CostEstimate(
            flops=6 * tokens * depth * units,
            bytes_accessed=6 * depth * units + 6 * tokens * units,
            transcendentals=0,
        ),
    )(x, in_t, gg, ug, hid)
    return grad_in, d_gate, d_up, d_down


def per_device(n_t, n_s, chunk, *args):
    inputs, out_grad, gate_pre = args[:3]
    rows, depth = inputs.shape
    tokens, units = gate_pre.shape
    n_q = n_t // 2
    fits = (
        n_t % 2 == 0
        and n_q == n_s
        and n_s > 1
        and depth % 256 == 0
        and out_grad.shape == (tokens // n_s, depth // 2)
        and out_grad.shape[0] % (16 * n_q) == 0
        and rows % 16 == 0
        and units % chunk == 0
        and units // chunk > 3
        and units * depth <= 8 * 1024 * 1024
        and tokens * units <= 1024 * 1024
    )
    if fits:
        return fused(n_q, n_s, chunk, *args)
    return plain(*args)


def solution(mesh, chunk=256):
    in_specs = (
        P("tp", "sp"),
        P("sp", "tp"),
        P(None, "tp"),
        P(None, "tp"),
        P("sp", "tp"),
        P("sp", "tp"),
        P("tp", "sp"),
    )
    out_specs = (P("tp", "sp"), P("sp", "tp"), P("sp", "tp"), P("tp", "sp"))
    return jax.shard_map(
        functools.partial(per_device, mesh.shape["tp"], mesh.shape["sp"], chunk),
        mesh=mesh, in_specs=in_specs, out_specs=out_specs, check_vma=False,
    )
```

```python
import functools

import jax
import jax.numpy as jnp
from jax import lax
from jax.experimental import pallas as pl
from jax.experimental.pallas import tpu as pltpu
from jax.sharding import PartitionSpec as P

BF = jnp.bfloat16
F32 = jnp.float32
MESH = pl.DeviceIdType.MESH
ANY = pl.BlockSpec(memory_space=pl.ANY)
VM = pl.BlockSpec(memory_space=pltpu.VMEM)
SLOTS = 4
SLACK = 2


def swiglu_back(hidden_grad, gate_pre, up_pre):
    gate = gate_pre.astype(F32)
    upward = up_pre.astype(F32)
    sigmoid = jax.nn.sigmoid(gate)
    up_grad = (hidden_grad * gate * sigmoid).astype(BF)
    gate_grad = (hidden_grad * upward * sigmoid * (1.0 + gate * (1.0 - sigmoid))).astype(BF)
    return (gate_grad, up_grad)


def rows_times(grads, weight):
    return lax.dot_general(grads, weight, (((1,), (1,)), ((), ())), preferred_element_type=F32)


def plain(inputs, out_grad, gate_pre, up_pre, w_gate, w_up, w_down):
    wide_rows = lax.all_gather(out_grad, "tp", axis=1, tiled=True)
    regrouped = lax.all_to_all(wide_rows, "sp", split_axis=1, concat_axis=0, tiled=True)
    gate = gate_pre.astype(F32)
    hidden = (gate * jax.nn.sigmoid(gate) * up_pre.astype(F32)).astype(BF)
    grad_down = lax.dot_general(
        hidden, regrouped, (((0,), (0,)), ((), ())), preferred_element_type=F32
    ).astype(BF)
    partial_grad = rows_times(regrouped, w_down)
    hidden_grad = lax.psum(partial_grad, "sp")
    gate_grad, up_grad = swiglu_back(hidden_grad, gate_pre, up_pre)
    dims = (((0,), (0,)), ((), ()))
    piece = lax.all_gather(inputs, "tp", axis=0, tiled=True)
    new_gate = lax.dot_general(piece, gate_grad, dims, preferred_element_type=F32)
    new_up = lax.dot_general(piece, up_grad, dims, preferred_element_type=F32)
    via_gate = lax.psum_scatter(
        rows_times(gate_grad, w_gate), "tp", scatter_dimension=0, tiled=True
    )
    via_up = lax.psum_scatter(rows_times(up_grad, w_up), "tp", scatter_dimension=0, tiled=True)
    total = via_gate + via_up
    return (total.astype(BF), new_gate.astype(BF), new_up.astype(BF), grad_down)


def first_kernel(
    n_q, n_s, chunk, n_c, tile,
    inputs, out_grad, gate_pre, up_pre, w_gate, w_up, w_down,
    grad_in, x_out, in_t_out, gg_out, ug_out, hid_out,
    quarter, x_all, x_flat, in_all, in_t, w_d, w_gu, part,
    from_l, from_r, to_r, to_l, gates, ups, swishes, slopes, gg, ug, hid, g_in, half_in, block_out, block_in,
    sem_a, sem_b, sem_c, sem_d, sem_i, sem_j, sem_h, sem_e,
    sem_wd, sem_w, sem_gu, sem_r, sem_l, sem_out, sem_x,
):
    t = lax.axis_index("tp")
    s = lax.axis_index("sp")
    q = t // 2
    k = lax.rem(t, 2)
    mate = t + 1 - 2 * k
    rows16 = quarter.shape[1]
    half = quarter.shape[2]
    depth = x_flat.shape[1]
    tokens = x_flat.shape[0]
    cols = pl.ds(pl.multiple_of(k * half, half), half)

    def wd_copy(j):
        return pltpu.make_async_copy(
            w_down.at[pl.ds(pl.multiple_of(j * chunk, chunk), chunk)], w_d.at[j], sem_wd.at[j]
        )

    def col(j):
        return pl.ds(pl.multiple_of(j * chunk, chunk), chunk)

    def w_copies(j):
        slot = lax.rem(j, SLOTS)
        return (
            pltpu.make_async_copy(
                w_gate.at[:, col(j)], w_gu.at[slot, :, pl.ds(0, chunk)], sem_w.at[0, slot]
            ),
            pltpu.make_async_copy(
                w_up.at[:, col(j)], w_gu.at[slot, :, pl.ds(chunk, chunk)], sem_w.at[1, slot]
            ),
        )

    def pre_copies(j):
        return (
            pltpu.make_async_copy(gate_pre.at[:, col(j)], gates.at[j], sem_gu.at[0, j]),
            pltpu.make_async_copy(up_pre.at[:, col(j)], ups.at[j], sem_gu.at[1, j]),
        )

    def out_copies(j):
        return (
            pltpu.make_async_copy(gg.at[j], gg_out.at[j], sem_out.at[0, j]),
            pltpu.make_async_copy(ug.at[j], ug_out.at[j], sem_out.at[1, j]),
        )

    def hid_copy(j):
        return pltpu.make_async_copy(hid.at[j], hid_out.at[j], sem_out.at[2, j])

    def remote(src, dst, sems, at, where):
        return pltpu.make_async_remote_copy(
            src_ref=src, dst_ref=dst, send_sem=sems.at[(0, *at)], recv_sem=sems.at[(1, *at)],
            device_id=where, device_id_type=MESH,
        )

    barrier = pltpu.get_barrier_semaphore()
    for o in range(1, n_q):
        pl.semaphore_signal(
            barrier, inc=1, device_id={"tp": lax.rem(q + o, n_q) * 2 + k}, device_id_type=MESH
        )
    for o in range(1, n_s):
        pl.semaphore_signal(
            barrier, inc=1, device_id={"sp": lax.rem(s + o, n_s)}, device_id_type=MESH
        )
    pl.semaphore_signal(barrier, inc=1, device_id={"tp": mate}, device_id_type=MESH)

    @pl.loop(0, n_c)
    def _(j):
        wd_copy(j).start()

    @pl.loop(0, n_c)
    def _(j):
        for c in pre_copies(j):
            c.start()

    pl.semaphore_wait(barrier, n_q + n_s - 1)

    def factors(f):
        for c in pre_copies(f):
            c.wait()
        gate = gates[f].astype(F32)
        upward = ups[f].astype(F32)
        sigmoid = 1.0 / (1.0 + jnp.exp(-gate))
        swish = gate * sigmoid
        swishes[f] = swish
        slopes[f] = upward * sigmoid * (1.0 + gate * (1.0 - sigmoid))
        hid[f] = (swish * upward).astype(BF).T
        hid_copy(f).start()

    stage = []
    for o in range(1, n_q):
        peer = lax.rem(q + o, n_q)
        stage.append(
            remote(
                out_grad.at[pl.ds(pl.multiple_of(peer * rows16, rows16), rows16)],
                quarter.at[q], sem_a, (o,), {"tp": peer * 2 + k},
            )
        )
        stage[-1].start()
    quarter[q] = out_grad[pl.ds(pl.multiple_of(q * rows16, rows16), rows16), :]
    for c in stage:
        c.wait()
    stage = []
    for o in range(1, n_s):
        peer = lax.rem(s + o, n_s)
        stage.append(
            remote(quarter.at[peer], x_all.at[s, q, :, cols], sem_b, (o,), {"sp": peer})
        )
        stage[-1].start()
    x_all[s, q, :, cols] = quarter[s]
    pl.loop(0, n_c // 2)(factors)
    for c in stage:
        c.wait()
    stage = []
    for o in range(1, n_q):
        peer = lax.rem(q + o, n_q)
        stage.append(
            remote(
                x_all.at[:, q, :, cols], x_all.at[:, q, :, cols], sem_c, (o,),
                {"tp": peer * 2 + k},
            )
        )
        stage[-1].start()

    for j in range(min(SLOTS, n_c)):
        for c in w_copies(j):
            c.start()
    pl.loop(n_c // 2, n_c)(factors)
    for c in stage:
        c.wait()
    swap = remote(x_all.at[:, :, :, cols], x_all.at[:, :, :, cols], sem_d, (0,), {"tp": mate})
    swap.start()
    in_stage = []
    for o in range(1, n_q):
        peer = lax.rem(q + o, n_q)
        in_stage.append(
            remote(inputs, in_all.at[q, k], sem_i, (o,), {"tp": peer * 2 + k})
        )
        in_stage[-1].start()
    in_all[q, k] = inputs[...]
    g_in[...] = jnp.zeros_like(g_in)
    swap.wait()
    x_flat[...] = x_all[...].reshape(tokens, depth)
    x_copy = pltpu.make_async_copy(x_flat, x_out, sem_x.at[0])
    x_copy.start()

    def send_r(j):
        return remote(
            to_r.at[j], from_l.at[j], sem_r, (j,), {"sp": jnp.minimum(s + 1, n_s - 1)}
        )

    def send_l(j):
        return remote(to_l.at[j], from_r.at[j], sem_l, (j,), {"sp": jnp.maximum(s - 1, 0)})

    def partial(j):
        wd_copy(j).wait()
        p = lax.dot_general(
            x_flat[...], w_d[j], (((1,), (1,)), ((), ())), preferred_element_type=F32
        )
        part[j] = p

        @pl.when(s == 0)
        def _():
            to_r[j] = p.astype(BF)
            send_r(j).start()
            from_l[j] = jnp.zeros((tokens, chunk), BF)

        @pl.when(s == n_s - 1)
        def _():
            to_l[j] = p.astype(BF)
            send_l(j).start()
            from_r[j] = jnp.zeros((tokens, chunk), BF)

    ahead = n_c // 2
    pl.loop(0, ahead)(partial)
    in_swap = remote(in_all.at[:, k], in_all.at[:, k], sem_j, (0,), {"tp": mate})
    lag = SLACK * jnp.maximum(s - 1, n_s - 2 - s)

    def finish(f):
        h = part[f] + from_l[f].astype(F32) + from_r[f].astype(F32)
        gg[f] = (h * slopes[f]).astype(BF)
        ug[f] = (h * swishes[f]).astype(BF)
        for c in out_copies(f):
            c.start()
        for c in w_copies(f):
            c.wait()
        slot = lax.rem(f, SLOTS)

        @pl.loop(0, depth // tile)
        def _(i):
            at = pl.ds(pl.multiple_of(i * tile, tile), tile)
            w = w_gu[slot, at, :]
            d = lax.dot_general(
                gg[f], w[:, :chunk], (((1,), (1,)), ((), ())), preferred_element_type=F32
            ) + lax.dot_general(
                ug[f], w[:, chunk:], (((1,), (1,)), ((), ())), preferred_element_type=F32
            )
            g_in[:, :, :, at] += d.reshape(n_q, 2, tokens // (2 * n_q), tile)

        @pl.when(f + SLOTS < n_c)
        def _():
            for c in w_copies(f + SLOTS):
                c.start()

    @pl.loop(0, n_c + SLACK * (n_s - 2))
    def _(step):
        cr = step - SLACK * (s - 1)
        cl = step - SLACK * (n_s - 2 - s)
        f = step - lag

        @pl.when((s > 0) & (cr >= 0) & (cr < n_c))
        def _():
            send_r(cr).wait_recv()

            @pl.when(s < n_s - 1)
            def _():
                to_r[cr] = (part[cr] + from_l[cr].astype(F32)).astype(BF)
                send_r(cr).start()

        @pl.when((s < n_s - 1) & (cl >= 0) & (cl < n_c))
        def _():
            send_l(cl).wait_recv()

            @pl.when(s > 0)
            def _():
                to_l[cl] = (part[cl] + from_r[cl].astype(F32)).astype(BF)
                send_l(cl).start()

        @pl.when(step < n_c - ahead)
        def _():
            partial(step + ahead)

        @pl.when(step == 1)
        def _():
            for c in in_stage:
                c.wait()
            in_swap.start()

        @pl.when((f >= 0) & (f < n_c))
        def _():
            finish(f)

        @pl.when(step == n_c // 2)
        def _():
            in_swap.wait()
            in_t[...] = in_all[...].reshape(tokens, depth).T
            pltpu.make_async_copy(in_t, in_t_out, sem_x.at[1]).start()

    pair = remote(g_in.at[:, 1 - k], half_in, sem_h, (0,), {"tp": mate})
    pair.start()
    pair.wait()
    stage = []
    for o in range(1, n_q):
        peer = lax.rem(q + o, n_q)
        block_out[o] = (g_in[peer, k] + half_in[peer]).astype(BF)
        stage.append(
            remote(block_out.at[o], block_in.at[o], sem_e, (o,), {"tp": peer * 2 + k})
        )
        stage[-1].start()
    total = g_in[q, k] + half_in[q]

    @pl.loop(0, n_c)
    def _(j):
        for c in out_copies(j):
            c.wait()
        hid_copy(j).wait()

        @pl.when(s < n_s - 1)
        def _():
            send_r(j).wait_send()

        @pl.when(s > 0)
        def _():
            send_l(j).wait_send()

    x_copy.wait()
    pltpu.make_async_copy(in_t, in_t_out, sem_x.at[1]).wait()
    for c in stage:
        c.wait()
    for o in range(1, n_q):
        total = total + block_in[o].astype(F32)
    grad_in[...] = total.astype(BF)


def second_kernel(n_sub, chunk, x, in_t, gg, ug, hid, d_gate, d_up, d_down):
    for c in range(n_sub):
        at = slice(c * chunk, (c + 1) * chunk)
        d_gate[:, at] = jnp.dot(in_t[...], gg[c], preferred_element_type=F32).astype(BF)
        d_up[:, at] = jnp.dot(in_t[...], ug[c], preferred_element_type=F32).astype(BF)
        d_down[at, :] = jnp.dot(hid[c], x[...], preferred_element_type=F32).astype(BF)


def fused(n_q, n_s, chunk, inputs, out_grad, gate_pre, up_pre, w_gate, w_up, w_down):
    rows, depth = inputs.shape
    tokens, units = gate_pre.shape
    n_c = units // chunk
    half = depth // 2
    rows16 = out_grad.shape[0] // n_q
    tile = min(512, depth)
    sds = jax.ShapeDtypeStruct
    dma = pltpu.SemaphoreType.DMA
    vm = pltpu.VMEM
    scratch = [
        vm((n_q, rows16, half), BF),
        vm((n_s, n_q, rows16, depth), BF),
        vm((tokens, depth), BF),
        vm((n_q, 2, rows, depth), BF),
        vm((depth, tokens), BF),
        vm((n_c, chunk, depth), BF),
        vm((SLOTS, depth, 2 * chunk), BF),
        vm((n_c, tokens, chunk), F32),
        vm((n_c, tokens, chunk), BF),
        vm((n_c, tokens, chunk), BF),
        vm((n_c, tokens, chunk), BF),
        vm((n_c, tokens, chunk), BF),
        vm((n_c, tokens, chunk), BF),
        vm((n_c, tokens, chunk), BF),
        vm((n_c, tokens, chunk), F32),
        vm((n_c, tokens, chunk), F32),
        vm((n_c, tokens, chunk), BF),
        vm((n_c, tokens, chunk), BF),
        vm((n_c, chunk, tokens), BF),
        vm((n_q, 2, rows, depth), F32),
        vm((n_q, rows, depth), F32),
        vm((n_q, rows, depth), BF),
        vm((n_q, rows, depth), BF),
        dma((2, n_q)),
        dma((2, n_s)),
        dma((2, n_q)),
        dma((2, 1)),
        dma((2, n_q)),
        dma((2, 1)),
        dma((2, 1)),
        dma((2, n_q)),
        dma((n_c,)),
        dma((2, SLOTS)),
        dma((2, n_c)),
        dma((2, n_c)),
        dma((2, n_c)),
        dma((3, n_c)),
        dma((2,)),
    ]
    grad_in, x, in_t, gg, ug, hid = pl.pallas_call(
        functools.partial(first_kernel, n_q, n_s, chunk, n_c, tile),
        out_shape=(
            sds((rows, depth), BF),
            sds((tokens, depth), BF),
            sds((depth, tokens), BF),
            sds((n_c, tokens, chunk), BF),
            sds((n_c, tokens, chunk), BF),
            sds((n_c, chunk, tokens), BF),
        ),
        in_specs=[VM, VM, ANY, ANY, ANY, ANY, ANY],
        out_specs=(VM, ANY, ANY, ANY, ANY, ANY),
        scratch_shapes=scratch,
        compiler_params=pltpu.CompilerParams(
            collective_id=0, has_side_effects=True, vmem_limit_bytes=60 * 1024 * 1024
        ),
        cost_estimate=pl.CostEstimate(
            flops=6 * tokens * depth * units,
            bytes_accessed=6 * depth * units + 14 * tokens * units,
            transcendentals=tokens * units,
        ),
    )(inputs, out_grad, gate_pre, up_pre, w_gate, w_up, w_down)

    n_sub = 2 if n_c % 2 == 0 else 1
    wide = n_sub * chunk
    whole = lambda i: (0, 0)
    d_gate, d_up, d_down = pl.pallas_call(
        functools.partial(second_kernel, n_sub, chunk),
        grid=(n_c // n_sub,),
        out_shape=(
            sds((depth, units), BF),
            sds((depth, units), BF),
            sds((units, depth), BF),
        ),
        in_specs=[
            pl.BlockSpec((tokens, depth), whole),
            pl.BlockSpec((depth, tokens), whole),
            pl.BlockSpec((n_sub, tokens, chunk), lambda i: (i, 0, 0)),
            pl.BlockSpec((n_sub, tokens, chunk), lambda i: (i, 0, 0)),
            pl.BlockSpec((n_sub, chunk, tokens), lambda i: (i, 0, 0)),
        ],
        out_specs=(
            pl.BlockSpec((depth, wide), lambda i: (0, i)),
            pl.BlockSpec((depth, wide), lambda i: (0, i)),
            pl.BlockSpec((wide, depth), lambda i: (i, 0)),
        ),
        compiler_params=pltpu.CompilerParams(vmem_limit_bytes=60 * 1024 * 1024),
        cost_estimate=pl.CostEstimate(
            flops=6 * tokens * depth * units,
            bytes_accessed=6 * depth * units + 6 * tokens * units,
            transcendentals=0,
        ),
    )(x, in_t, gg, ug, hid)
    return grad_in, d_gate, d_up, d_down


def per_device(n_t, n_s, chunk, *args):
    inputs, out_grad, gate_pre = args[:3]
    rows, depth = inputs.shape
    tokens, units = gate_pre.shape
    n_q = n_t // 2
    fits = (
        n_t % 2 == 0
        and n_q == n_s
        and n_s > 1
        and depth % 256 == 0
        and out_grad.shape == (tokens // n_s, depth // 2)
        and out_grad.shape[0] % (16 * n_q) == 0
        and rows % 16 == 0
        and units % chunk == 0
        and units // chunk > 3
        and units * depth <= 8 * 1024 * 1024
        and tokens * units <= 1024 * 1024
    )
    if fits:
        return fused(n_q, n_s, chunk, *args)
    return plain(*args)


def solution(mesh, chunk=256):
    in_specs = (
        P("tp", "sp"),
        P("sp", "tp"),
        P(None, "tp"),
        P(None, "tp"),
        P("sp", "tp"),
        P("sp", "tp"),
        P("tp", "sp"),
    )
    out_specs = (P("tp", "sp"), P("sp", "tp"), P("sp", "tp"), P("tp", "sp"))
    return jax.shard_map(
        functools.partial(per_device, mesh.shape["tp"], mesh.shape["sp"], chunk),
        mesh=mesh, in_specs=in_specs, out_specs=out_specs, check_vma=False,
    )
```
